768 devices in a mesh: dp: 32 (over y_hi, x, core), mp: 24 (over y_lo, z).
Axes of the slice: x: 4, y: 8 (y_hi: 4, y_lo: 2; y = y_hi * 2 + y_lo), z: 12, core: 2. Of those that a mesh axis runs over, the one named last changes fastest.
Arguments:
- img_feat: bfloat16 [16384, 1152], P('dp'), may hold values from -6 to 6
- txt_feat: bfloat16 [16384, 1152], P('dp'), may hold values from -6 to 6
- img_head: bfloat16 [1152, 1152], P(None, 'mp'), may hold values from -0.1875 to 0.1875
- txt_head: bfloat16 [1152, 1152], P(None, 'mp'), may hold values from -0.1875 to 0.1875
- partner: int32 [16384], P('dp'), may hold values from 0 to 511
- log_scale: float32 [1], replicated, may hold values from 1.5 to 2.5
- logit_bias: float32 [1], replicated, may hold values from -8 to -4
- loss_scale: float32 [1], replicated, may hold values from 8192 to 16384
Outputs:
- img_head_grad: float32 [1152, 1152], P(None, 'mp')
- txt_head_grad: float32 [1152, 1152], P(None, 'mp')
The draws below stay inside these ranges and needn't reach their ends.
Inputs may be any that keep to these rules, and one draw needn't show every extreme that they name: Image i's positive text is row partner[i] of the same block of 512 pairs.
All inputs are finite; a program needn't handle non-finite values.
Results may differ from the reference program's by a relative error of at most 0.0059.
Values may be sent and summed in bfloat16 or wider, within the bound.
No kernel may reach another device: no remote copies, remote signals or barrier semaphores. Data moves between devices by JAX's collectives and lax.ppermute only.
A program may use at most 32 MiB of HBM per device.

```python
import jax
import jax.numpy as jnp
from jax import lax

D = 1152
E = 1152
ROWS = 512
STEPS = 2
BLOCKS = 32
TOKENS = 16384


def plant(result, rng, low, top_value):
    spot = [jax.random.randint(jax.random.fold_in(rng, axis), (), 0, length) for axis, length in enumerate(result.shape)]
    longest = result.shape.index(max(result.shape))
    next_to = spot[:longest] + [(spot[longest] + 1) % result.shape[longest]] + spot[longest + 1:]
    return result.at[tuple(spot)].set(low).at[tuple(next_to)].set(top_value)


def levels(rng, dims, split, smallest, largest):
    def one(axis_at, shards_of):
        heights = jax.random.uniform(jax.random.fold_in(jax.random.fold_in(rng, 6), axis_at), (shards_of,), jnp.float32, smallest / len(split), largest / len(split))
        return jnp.repeat(jnp.exp(heights), dims[axis_at] // shards_of).reshape((-1,) + (1,) * (len(dims) - axis_at - 1))

    factor_of = one(*split[0])
    for cut in split[1:]:
        factor_of = factor_of * one(*cut)
    return factor_of


def scatter_about(key, extent, scale, bound, cuts=(), kind=jnp.bfloat16):
    loudness = levels(key, extent, cuts, -0.22, 0.18) if cuts else 1.0
    values = jax.random.normal(key, extent, jnp.float32) * scale * loudness
    return jnp.minimum(jnp.maximum(values, -bound), bound).astype(kind)


def setup_inputs(seed: int = 0) -> dict:
    splits = jax.random.split(jax.random.key(seed), 9)
    return {
        "img_feat": scatter_about(splits[0], (TOKENS, D), 1.0, 6.0, ((0, 32),)),
        "txt_feat": scatter_about(splits[1], (TOKENS, D), 1.0, 6.0, ((0, 32),)),
        "img_head": scatter_about(splits[2], (D, E), D ** -0.5, 0.1875, ((1, 24),)),
        "txt_head": scatter_about(splits[3], (D, E), D ** -0.5, 0.1875, ((1, 24),)),
        "partner": plant(jax.random.randint(splits[4], (TOKENS,), 0, ROWS), jax.random.fold_in(splits[4], 1), 0, ROWS - 1).astype(jnp.int32),
        "log_scale": jnp.clip(jax.random.uniform(splits[5], (1,), jnp.float32, 1.5, 2.5), 1.5, 2.5),
        "logit_bias": jnp.clip(jax.random.uniform(splits[6], (1,), jnp.float32, -8.0, -4.0), -8.0, -4.0),
        "loss_scale": jnp.clip(jax.random.uniform(splits[7], (1,), jnp.float32, 8192.0, 16384.0), 8192.0, 16384.0),
    }


norm_epsilon = 1e-06

def reference(img_feat, txt_feat, img_head, txt_head, partner, log_scale, logit_bias, loss_scale):
    img_proj = jnp.dot(img_feat, img_head, preferred_element_type=jnp.float32)
    txt_proj = jnp.dot(txt_feat, txt_head, preferred_element_type=jnp.float32)
    img_norm = jnp.sqrt(lax.optimization_barrier(jnp.sum(img_proj * img_proj, 1)) + norm_epsilon)
    txt_norm = jnp.sqrt(lax.optimization_barrier(jnp.sum(txt_proj * txt_proj, 1)) + norm_epsilon)
    img_unit = img_proj / img_norm[:, None]
    txt_unit = txt_proj / txt_norm[:, None]
    img_emb = img_unit.astype(jnp.bfloat16)
    txt_emb = txt_unit.astype(jnp.bfloat16)
    temper = jnp.exp(log_scale[0])
    offset = logit_bias[0]
    weight = loss_scale[0] / TOKENS
    img_blocks = img_emb.astype(jnp.float32).reshape(BLOCKS, ROWS, E)
    txt_blocks = txt_emb.astype(jnp.float32).reshape(BLOCKS, ROWS, E)
    pair_blocks = partner.reshape(BLOCKS, ROWS)
    positive = jnp.arange(ROWS, dtype=jnp.int32)[None, None, :] == pair_blocks[:, :, None]
    img_grad = jnp.zeros((BLOCKS, ROWS, E), jnp.float32)
    img_radial = jnp.zeros((BLOCKS, ROWS), jnp.float32)
    txt_grad = jnp.zeros((BLOCKS, ROWS, E), jnp.bfloat16)
    txt_radial = jnp.zeros((BLOCKS, ROWS), jnp.bfloat16)
    for step in range(STEPS):
        txt_here = jnp.roll(txt_blocks, step, axis=0)
        sims = jnp.einsum('pre,pqe->prq', img_blocks, txt_here)
        logits = temper * sims + offset
        if step == 0:
            signs = jnp.where(positive, 1.0, -1.0).astype(jnp.float32)
            coef = (-signs * jax.nn.sigmoid(-signs * logits) * weight).astype(jnp.bfloat16)
        else:
            coef = (jax.nn.sigmoid(logits) * weight).astype(jnp.bfloat16)
        coef_wide = coef.astype(jnp.float32)
        weighted = coef_wide * sims
        img_grad = img_grad + temper * jnp.einsum('prq,pqe->pre', coef_wide, txt_here)
        img_radial = img_radial + temper * lax.optimization_barrier(jnp.sum(weighted, 2))
        txt_term = temper * jnp.einsum('prq,pre->pqe', coef_wide, img_blocks)
        rad_term = temper * lax.optimization_barrier(jnp.sum(weighted, 1))
        txt_grad = (txt_grad.astype(jnp.float32) + jnp.roll(txt_term, -step, axis=0)).astype(jnp.bfloat16)
        txt_radial = (txt_radial.astype(jnp.float32) + jnp.roll(rad_term, -step, axis=0)).astype(jnp.bfloat16)
    img_grad = img_grad.reshape(TOKENS, E)
    img_radial = img_radial.reshape(TOKENS)
    txt_grad = txt_grad.astype(jnp.float32).reshape(TOKENS, E)
    txt_radial = txt_radial.astype(jnp.float32).reshape(TOKENS)
    img_dproj = ((img_grad - img_unit * img_radial[:, None]) / img_norm[:, None]).astype(jnp.bfloat16)
    txt_dproj = ((txt_grad - txt_unit * txt_radial[:, None]) / txt_norm[:, None]).astype(jnp.bfloat16)
    img_head_grad = jnp.dot(img_feat.T, img_dproj, preferred_element_type=jnp.float32)
    txt_head_grad = jnp.dot(txt_feat.T, txt_dproj, preferred_element_type=jnp.float32)
    return (img_head_grad, txt_head_grad)
```

```python
import jax
import jax.numpy as jnp
from jax import lax
from jax.sharding import Mesh, PartitionSpec as P

norm_epsilon = 1e-06

DP = ("yh", "x", "core")
MP = ("yl", "z")
SIZES = {"yh": 4, "x": 4, "core": 2, "yl": 2, "z": 12}

WIRE_SCALE = 32.0


def dot(left, right, left_dim, right_dim):
    return lax.dot_general(
        left, right, (((left_dim,), (right_dim,)), ((), ())), preferred_element_type=jnp.float32
    )


def to_block(value, distance):
    count = lax.axis_size(DP)
    return lax.ppermute(value, DP, [(i, (i + distance) % count) for i in range(count)])


def swapped(value):
    return lax.ppermute(value, "yl", [(0, 1), (1, 0)])


def shards(img_feat, txt_feat, img_head, txt_head, partner, log_scale, logit_bias, loss_scale):
    rows = img_feat.shape[0]
    cols = img_head.shape[1]
    half = rows // 2
    blocks = lax.axis_size(DP)
    side = lax.axis_index("yl")
    temper = jnp.exp(log_scale[0])
    offset = logit_bias[0]
    weight = loss_scale[0] / (rows * blocks)

    img_proj = dot(img_head, img_feat, 0, 1)
    txt_proj = dot(txt_head, txt_feat, 0, 1)
    img_wire = (img_proj * WIRE_SCALE).astype(jnp.float16)
    txt_wire = (txt_proj * WIRE_SCALE).astype(jnp.float16)
    txt_mine = jnp.where(side == 0, txt_wire[:, :half], txt_wire[:, half:])
    txt_theirs = jnp.where(side == 0, txt_wire[:, half:], txt_wire[:, :half])

    other = swapped(jnp.concatenate([img_wire, txt_theirs], 1))
    txt_pair = jnp.concatenate([txt_mine, other[:, rows:]], 0)
    before = to_block(txt_pair, 1)
    img_pair = jnp.concatenate([img_wire, other[:, :rows]], 0)
    pair = jnp.concatenate([img_pair, txt_pair, before], 1)
    whole = lax.all_gather(pair, "z", axis=0, tiled=True).astype(jnp.float32)

    square = jnp.sum(whole * whole, 0) * (1.0 / WIRE_SCALE**2)
    norm = jnp.sqrt(square + norm_epsilon)
    shrink = 1.0 / (norm * WIRE_SCALE)
    emb = (whole * shrink[None, :]).astype(jnp.bfloat16)
    near = (pair.astype(jnp.float32) * shrink[None, :]).astype(jnp.bfloat16)

    sims = dot(emb[:, :rows], emb[:, rows:], 0, 0)
    place = lax.broadcasted_iota(jnp.int32, (rows, rows), 1)
    positive = (place + side * half == partner[:, None]) & (place < half)
    signs = jnp.where(positive, -1.0, 1.0).astype(jnp.float32)
    coef = (signs * jax.nn.sigmoid(signs * (temper * sims + offset)) * weight).astype(jnp.bfloat16)
    weighted = coef.astype(jnp.float32) * sims
    img_radial = temper * jnp.sum(weighted, 1)
    txt_radial = temper * jnp.sum(weighted, 0)
    img_grad = temper * dot(near[:, rows:], coef, 1, 1)
    txt_grad = temper * dot(near[:, :rows], coef, 1, 0)

    back = jnp.concatenate([txt_grad[:, half:], txt_radial[None, half:]], 0).astype(jnp.bfloat16)
    back = to_block(back, -1).astype(jnp.float32)
    txt_sum = txt_grad[:, :half].astype(jnp.bfloat16).astype(jnp.float32) + back[: 2 * cols]
    txt_sum = txt_sum.astype(jnp.bfloat16).astype(jnp.float32)
    rad_sum = txt_radial[:half].astype(jnp.bfloat16).astype(jnp.float32) + back[2 * cols]
    rad_sum = rad_sum.astype(jnp.bfloat16).astype(jnp.float32)

    txt_norm = norm[rows : rows + half]
    give = jnp.concatenate(
        [
            jnp.concatenate([img_grad[cols:], img_radial[None, :]], 0),
            jnp.concatenate([txt_sum[cols:], rad_sum[None, :]], 0),
        ],
        1,
    )
    give = jnp.concatenate([give, jnp.pad(txt_norm, (0, rows))[None, :]], 0)
    got = swapped(give)
    img_grad = img_grad[:cols] + got[:cols, :rows]
    img_radial = img_radial + got[cols, :rows]

    def both(mine, theirs):
        first = jnp.where(side == 0, mine, theirs)
        second = jnp.where(side == 0, theirs, mine)
        return jnp.concatenate([first, second], mine.ndim - 1)

    txt_grad = both(txt_sum[:cols], got[:cols, rows:])
    txt_radial = both(rad_sum, got[cols, rows:])
    txt_norm = both(txt_norm, got[cols + 1, :half])
    img_norm = norm[:rows]

    def head_part(feat, grad, proj, radial, norm):
        unit = proj / norm[None, :]
        dproj = ((grad - unit * radial[None, :]) / norm[None, :]).astype(jnp.bfloat16)
        return dot(dproj, feat, 1, 0)

    part = jnp.concatenate(
        [
            head_part(img_feat, img_grad, img_proj, img_radial, img_norm),
            head_part(txt_feat, txt_grad, txt_proj, txt_radial, txt_norm),
        ],
        0,
    )
    share = part.reshape(blocks, 2 * cols // blocks, -1)
    share = jnp.sum(lax.all_to_all(share, DP, 0, 0, tiled=True), 0).astype(jnp.bfloat16)
    share = jnp.broadcast_to(share[None], (blocks,) + share.shape)
    total = lax.all_to_all(share, DP, 0, 0, tiled=True)
    total = total.astype(jnp.float32).reshape(2 * cols, -1)
    return (total[:cols].T, total[cols:].T)


def solution(mesh):
    lines = Mesh(mesh.devices.reshape(tuple(SIZES.values())), tuple(SIZES))
    return jax.shard_map(
        shards,
        mesh=lines,
        in_specs=(P(DP, None), P(DP, None), P(None, MP), P(None, MP), P(DP), P(), P(), P()),
        out_specs=(P(None, MP), P(None, MP)),
        check_vma=False,
    )
```

```python
import jax
import jax.numpy as jnp
from jax import lax
from jax.sharding import Mesh, PartitionSpec as P

norm_epsilon = 1e-06

DP = ("yh", "x", "core")
MP = ("yl", "z")
SIZES = {"yh": 4, "x": 4, "core": 2, "yl": 2, "z": 12}

WIRE_SCALE = 32.0


def dot(left, right, left_dim, right_dim):
    return lax.dot_general(
        left, right, (((left_dim,), (right_dim,)), ((), ())), preferred_element_type=jnp.float32
    )


def swapped(value, axis):
    return lax.ppermute(value, axis, [(0, 1), (1, 0)])


def from_all(value, axes, routes):
    return lax.ppermute(value, axes, [(b * 2 + s, c * 2 + t) for (b, s), (c, t) in routes])


def shards(img_feat, txt_feat, img_head, txt_head, partner, log_scale, logit_bias, loss_scale):
    rows = img_feat.shape[0]
    cols = img_head.shape[1]
    blocks = lax.axis_size(DP)
    group = lax.axis_size(("yh", "x"))
    side = lax.axis_index("yl")
    core = lax.axis_index("core")
    temper = jnp.exp(log_scale[0])
    offset = logit_bias[0]
    weight = loss_scale[0] / (rows * blocks)

    img_wire = (dot(img_head, img_feat, 0, 1) * WIRE_SCALE).astype(jnp.float16)
    txt_wire = (dot(txt_head, txt_feat, 0, 1) * WIRE_SCALE).astype(jnp.float16)

    around = [(b, (b + 1) % blocks) for b in range(blocks)]
    axes = DP + ("yl",)
    img_other = swapped(img_wire, "yl")
    txt_other = from_all(
        txt_wire,
        axes,
        [((b, 1), (b, 0)) for b in range(blocks)] + [((b, 0), (c, 1)) for b, c in around],
    )
    txt_before = from_all(txt_wire, axes, [((b, 1), (c, 1)) for b, c in around])
    txt_first = jnp.where(side == 0, txt_wire, txt_before)
    pair = jnp.concatenate(
        [
            jnp.concatenate([img_wire, img_other], 0),
            jnp.concatenate([txt_first, txt_other], 0),
        ],
        1,
    )
    pair, late_feat = lax.optimization_barrier((pair, txt_feat))
    feat_before = lax.ppermute(late_feat, DP, around)
    whole = lax.all_gather(pair, "z", axis=0, tiled=True)
    whole, feat_before = lax.optimization_barrier((whole, feat_before))
    whole = whole.astype(jnp.float32)

    square = jnp.sum(whole * whole, 0) * (1.0 / WIRE_SCALE**2)
    norm = jnp.sqrt(square + norm_epsilon)
    shrink = 1.0 / (norm * WIRE_SCALE)
    emb = (whole * shrink[None, :]).astype(jnp.bfloat16)
    unit = pair.astype(jnp.float32) * shrink[None, :]
    near = unit.astype(jnp.bfloat16)

    sims = dot(emb[:, :rows], emb[:, rows:], 0, 0)
    place = lax.broadcasted_iota(jnp.int32, (rows, rows), 1)
    positive = (place == partner[:, None]) & (side == 0)
    signs = jnp.where(positive, -1.0, 1.0).astype(jnp.float32)
    coef = (signs * jax.nn.sigmoid(signs * (temper * sims + offset)) * weight).astype(jnp.bfloat16)
    weighted = coef.astype(jnp.float32) * sims
    radial = temper * jnp.concatenate([jnp.sum(weighted, 1), jnp.sum(weighted, 0)])
    grad = temper * jnp.concatenate(
        [dot(near[:, rows:], coef, 1, 1), dot(near[:, :rows], coef, 1, 0)], 1
    )
    dproj = (grad - unit * radial[None, :]) / norm[None, :]
    got = swapped(dproj[cols:].astype(jnp.bfloat16), "yl")
    mine = dproj[:cols]
    img_dproj = (mine[:, :rows] + got[:, :rows].astype(jnp.float32)).astype(jnp.bfloat16)
    txt_mine, txt_got = mine[:, rows:].astype(jnp.bfloat16), got[:, rows:]
    txt_dproj = jnp.where(side == 0, txt_mine, txt_got)
    txt_dproj_before = jnp.where(side == 0, txt_got, txt_mine)

    img_part = dot(img_dproj, img_feat, 1, 0)
    txt_part = dot(txt_dproj, txt_feat, 1, 0) + dot(txt_dproj_before, feat_before, 1, 0)

    kept = jnp.where(core == 0, img_part, txt_part)
    kept = kept + swapped(jnp.where(core == 0, txt_part, img_part), "core")
    share = kept.reshape(group, cols // group, -1)
    share = jnp.sum(lax.all_to_all(share, ("yh", "x"), 0, 0, tiled=True), 0).astype(jnp.bfloat16)
    share = jnp.broadcast_to(share[None], (group,) + share.shape)
    total = lax.all_to_all(share, ("yh", "x"), 0, 0, tiled=True).reshape(cols, -1)
    other = swapped(total, "core")
    img_total = jnp.where(core == 0, total, other).astype(jnp.float32)
    txt_total = jnp.where(core == 0, other, total).astype(jnp.float32)
    return (img_total.T, txt_total.T)


def solution(mesh):
    lines = Mesh(mesh.devices.reshape(tuple(SIZES.values())), tuple(SIZES))
    return jax.shard_map(
        shards,
        mesh=lines,
        in_specs=(P(DP, None), P(DP, None), P(None, MP), P(None, MP), P(DP), P(), P(), P()),
        out_specs=(P(None, MP), P(None, MP)),
        check_vma=False,
    )
```

```python
import jax
import jax.numpy as jnp
from jax import lax
from jax.sharding import Mesh, PartitionSpec as P

norm_epsilon = 1e-06

DP = ("yh", "x", "core")
MP = ("yl", "z")
SIZES = {"yh": 4, "x": 4, "core": 2, "yl": 2, "z": 12}

WIRE_SCALE = 32.0


def dot(left, right, left_dim, right_dim):
    return lax.dot_general(
        left, right, (((left_dim,), (right_dim,)), ((), ())), preferred_element_type=jnp.float32
    )


def swapped(value, axis):
    return lax.ppermute(value, axis, [(0, 1), (1, 0)])


def from_all(value, axes, routes):
    return lax.ppermute(value, axes, [(b * 2 + s, c * 2 + t) for (b, s), (c, t) in routes])


def shards(img_feat, txt_feat, img_head, txt_head, partner, log_scale, logit_bias, loss_scale):
    rows = img_feat.shape[0]
    cols = img_head.shape[1]
    blocks = lax.axis_size(DP)
    side = lax.axis_index("yl")
    temper = jnp.exp(log_scale[0])
    offset = logit_bias[0]
    weight = loss_scale[0] / (rows * blocks)

    img_wire = (dot(img_head, img_feat, 0, 1) * WIRE_SCALE).astype(jnp.float16)
    txt_wire = (dot(txt_head, txt_feat, 0, 1) * WIRE_SCALE).astype(jnp.float16)

    around = [(b, (b + 1) % blocks) for b in range(blocks)]
    axes = DP + ("yl",)
    img_other = swapped(img_wire, "yl")
    txt_other = from_all(
        txt_wire,
        axes,
        [((b, 1), (b, 0)) for b in range(blocks)] + [((b, 0), (c, 1)) for b, c in around],
    )
    txt_before = from_all(txt_wire, axes, [((b, 1), (c, 1)) for b, c in around])
    txt_first = jnp.where(side == 0, txt_wire, txt_before)
    pair = jnp.concatenate(
        [
            jnp.concatenate([img_wire, img_other], 0),
            jnp.concatenate([txt_first, txt_other], 0),
        ],
        1,
    )
    whole = lax.all_gather(pair, "z", axis=0, tiled=True).astype(jnp.float32)

    square = jnp.sum(whole * whole, 0) * (1.0 / WIRE_SCALE**2)
    norm = jnp.sqrt(square + norm_epsilon)
    shrink = 1.0 / (norm * WIRE_SCALE)
    emb = (whole * shrink[None, :]).astype(jnp.bfloat16)
    unit = pair.astype(jnp.float32) * shrink[None, :]
    near = unit.astype(jnp.bfloat16)

    sims = dot(emb[:, :rows], emb[:, rows:], 0, 0)
    place = lax.broadcasted_iota(jnp.int32, (rows, rows), 1)
    positive = (place == partner[:, None]) & (side == 0)
    signs = jnp.where(positive, -1.0, 1.0).astype(jnp.float32)
    coef = (signs * jax.nn.sigmoid(signs * (temper * sims + offset)) * weight).astype(jnp.bfloat16)
    weighted = coef.astype(jnp.float32) * sims
    radial = temper * jnp.concatenate([jnp.sum(weighted, 1), jnp.sum(weighted, 0)])
    def head_side(grad, at):
        part = temper * grad - unit[:, at] * radial[None, at]
        return part / norm[None, at]

    txt_term = head_side(dot(near[:, :rows], coef, 1, 0), slice(rows, None)).astype(jnp.bfloat16)
    img_term = head_side(dot(near[:, rows:], coef, 1, 1), slice(0, rows))

    txt_away = from_all(
        txt_term[cols:],
        axes,
        [((b, 0), (b, 1)) for b in range(blocks)] + [((c, 1), (b, 0)) for b, c in around],
    )
    txt_after = from_all(txt_term[:cols], axes, [((c, 1), (b, 1)) for b, c in around])
    img_away = swapped(img_term[cols:].astype(jnp.bfloat16), "yl")
    img_dproj = (img_term[:cols] + img_away.astype(jnp.float32)).astype(jnp.bfloat16)
    txt_own = jnp.where(side == 0, txt_term[:cols], txt_after)
    txt_dproj = (txt_own.astype(jnp.float32) + txt_away.astype(jnp.float32)).astype(jnp.bfloat16)

    part = jnp.concatenate([dot(img_dproj, img_feat, 1, 0), dot(txt_dproj, txt_feat, 1, 0)], 0)

    near_by = ("x", "core")
    count, far = lax.axis_size(near_by), lax.axis_size("yh")
    share = part.astype(jnp.bfloat16).reshape(count, 2 * cols // count, -1)
    share = lax.all_to_all(share, near_by, 0, 0, tiled=True)
    share = jnp.sum(share.astype(jnp.float32), 0)
    share = jnp.broadcast_to(share[None], (far,) + share.shape)
    share = jnp.sum(lax.all_to_all(share, "yh", 0, 0, tiled=True), 0).astype(jnp.bfloat16)
    share = jnp.broadcast_to(share[None], (count,) + share.shape)
    total = lax.all_to_all(share, near_by, 0, 0, tiled=True)
    total = total.astype(jnp.float32).reshape(2 * cols, -1)
    return (total[:cols].T, total[cols:].T)


def solution(mesh):
    lines = Mesh(mesh.devices.reshape(tuple(SIZES.values())), tuple(SIZES))
    return jax.shard_map(
        shards,
        mesh=lines,
        in_specs=(P(DP, None), P(DP, None), P(None, MP), P(None, MP), P(DP), P(), P(), P()),
        out_specs=(P(None, MP), P(None, MP)),
        check_vma=False,
    )
```

```python
import jax
import jax.numpy as jnp
from jax import lax
from jax.sharding import Mesh, PartitionSpec as P

norm_epsilon = 1e-06

DP = ("yh", "x", "core")
MP = ("yl", "z")
SIZES = {"yh": 4, "x": 4, "core": 2, "yl": 2, "z": 12}

WIRE_SCALE = 32.0


def dot(left, right, left_dim, right_dim):
    return lax.dot_general(
        left, right, (((left_dim,), (right_dim,)), ((), ())), preferred_element_type=jnp.float32
    )


def swapped(value, axis):
    return lax.ppermute(value, axis, [(0, 1), (1, 0)])


def from_all(value, axes, routes):
    return lax.ppermute(value, axes, [(b * 2 + s, c * 2 + t) for (b, s), (c, t) in routes])


def shards(img_feat, txt_feat, img_head, txt_head, partner, log_scale, logit_bias, loss_scale):
    rows = img_feat.shape[0]
    cols = img_head.shape[1]
    blocks = lax.axis_size(DP)
    side = lax.axis_index("yl")
    temper = jnp.exp(log_scale[0])
    offset = logit_bias[0]
    weight = loss_scale[0] / (rows * blocks)

    img_wire = (dot(img_head, img_feat, 0, 1) * WIRE_SCALE).astype(jnp.float16)
    txt_wire = (dot(txt_head, txt_feat, 0, 1) * WIRE_SCALE).astype(jnp.float16)

    around = [(b, (b + 1) % blocks) for b in range(blocks)]
    axes = DP + ("yl",)
    img_other = swapped(img_wire, "yl")
    txt_other = from_all(
        txt_wire,
        axes,
        [((b, 1), (b, 0)) for b in range(blocks)] + [((b, 0), (c, 1)) for b, c in around],
    )
    txt_before = from_all(txt_wire, axes, [((b, 1), (c, 1)) for b, c in around])
    txt_first = jnp.where(side == 0, txt_wire, txt_before)
    pair = jnp.concatenate(
        [
            jnp.concatenate([img_wire, img_other], 0),
            jnp.concatenate([txt_first, txt_other], 0),
        ],
        1,
    )
    whole = lax.all_gather(pair, "z", axis=0, tiled=True).astype(jnp.float32)

    square = jnp.sum(whole * whole, 0) * (1.0 / WIRE_SCALE**2)
    norm = jnp.sqrt(square + norm_epsilon)
    shrink = 1.0 / (norm * WIRE_SCALE)
    emb = (whole * shrink[None, :]).astype(jnp.bfloat16)
    unit = pair.astype(jnp.float32) * shrink[None, :]
    near = unit.astype(jnp.bfloat16)

    sims = dot(emb[:, :rows], emb[:, rows:], 0, 0)
    place = lax.broadcasted_iota(jnp.int32, (rows, rows), 1)
    positive = (place == partner[:, None]) & (side == 0)
    signs = jnp.where(positive, -1.0, 1.0).astype(jnp.float32)
    coef = (signs * jax.nn.sigmoid(signs * (temper * sims + offset)) * weight).astype(jnp.bfloat16)
    weighted = coef.astype(jnp.float32) * sims
    radial = temper * jnp.concatenate([jnp.sum(weighted, 1), jnp.sum(weighted, 0)])
    def head_side(grad, at):
        part = temper * grad - unit[:, at] * radial[None, at]
        return part / norm[None, at]

    txt_term = head_side(dot(near[:, :rows], coef, 1, 0), slice(rows, None)).astype(jnp.bfloat16)
    txt_away = from_all(
        txt_term[cols:],
        axes,
        [((b, 0), (b, 1)) for b in range(blocks)] + [((c, 1), (b, 0)) for b, c in around],
    )
    txt_after = from_all(txt_term[:cols], axes, [((c, 1), (b, 1)) for b, c in around])
    later, _ = lax.optimization_barrier((coef, txt_term))
    img_term = head_side(dot(near[:, rows:], later, 1, 1), slice(0, rows)).astype(jnp.bfloat16)
    img_away = swapped(img_term[cols:], "yl")
    txt_own = jnp.where(side == 0, txt_term[:cols], txt_after)

    img_part = dot(img_term[:cols], img_feat, 1, 0) + dot(img_away, img_feat, 1, 0)
    txt_part = dot(txt_own, txt_feat, 1, 0) + dot(txt_away, txt_feat, 1, 0)
    part = jnp.concatenate([img_part, txt_part], 0)

    near_by = ("x", "core")
    count, far = lax.axis_size(near_by), lax.axis_size("yh")
    share = part.astype(jnp.bfloat16).reshape(count, 2 * cols // count, -1)
    share = lax.all_to_all(share, near_by, 0, 0, tiled=True)
    share = jnp.sum(share.astype(jnp.float32), 0).astype(jnp.bfloat16)
    share = jnp.broadcast_to(share[None], (far,) + share.shape)
    share = lax.all_to_all(share, "yh", 0, 0, tiled=True)
    share = jnp.sum(share.astype(jnp.float32), 0).astype(jnp.bfloat16)
    share = jnp.broadcast_to(share[None], (count,) + share.shape)
    total = lax.all_to_all(share, near_by, 0, 0, tiled=True)
    total = lax.optimization_barrier(total.reshape(2 * cols, -1)).astype(jnp.float32)
    return (total[:cols].T, total[cols:].T)


def solution(mesh):
    lines = Mesh(mesh.devices.reshape(tuple(SIZES.values())), tuple(SIZES))
    return jax.shard_map(
        shards,
        mesh=lines,
        in_specs=(P(DP, None), P(DP, None), P(None, MP), P(None, MP), P(DP), P(), P(), P()),
        out_specs=(P(None, MP), P(None, MP)),
        check_vma=False,
    )
```

```python
import jax
import jax.numpy as jnp
from jax import lax
from jax.sharding import Mesh, PartitionSpec as P

norm_epsilon = 1e-06

DP = ("yh", "x", "core")
MP = ("yl", "z")
SIZES = {"yh": 4, "x": 4, "core": 2, "yl": 2, "z": 12}

WIRE_SCALE = 32.0


def dot(left, right, left_dim, right_dim):
    return lax.dot_general(
        left, right, (((left_dim,), (right_dim,)), ((), ())), preferred_element_type=jnp.float32
    )


def swapped(value, axis):
    return lax.ppermute(value, axis, [(0, 1), (1, 0)])


def from_all(value, axes, routes):
    return lax.ppermute(value, axes, [(b * 2 + s, c * 2 + t) for (b, s), (c, t) in routes])


def shards(img_feat, txt_feat, img_head, txt_head, partner, log_scale, logit_bias, loss_scale):
    rows = img_feat.shape[0]
    cols = img_head.shape[1]
    blocks = lax.axis_size(DP)
    side = lax.axis_index("yl")
    temper = jnp.exp(log_scale[0])
    offset = logit_bias[0]
    weight = loss_scale[0] / (rows * blocks)

    img_wire = (dot(img_head, img_feat, 0, 1) * WIRE_SCALE).astype(jnp.float16)
    txt_wire = (dot(txt_head, txt_feat, 0, 1) * WIRE_SCALE).astype(jnp.float16)

    around = [(b, (b + 1) % blocks) for b in range(blocks)]
    axes = DP + ("yl",)
    feat_there = from_all(
        txt_feat,
        axes,
        [((b, 0), (b, 0)) for b in range(blocks)] + [((b, 1), (c, 1)) for b, c in around],
    )
    txt_other = from_all(
        txt_wire,
        axes,
        [((b, 1), (b, 0)) for b in range(blocks)] + [((b, 0), (c, 1)) for b, c in around],
    )
    txt_before = from_all(txt_wire, axes, [((b, 1), (c, 1)) for b, c in around])
    img_other = swapped(img_wire, "yl")
    txt_first = jnp.where(side == 0, txt_wire, txt_before)

    near_by = ("x", "core")
    count, far = lax.axis_size(near_by), lax.axis_size(("yh", "yl"))
    piece = 2 * cols // count

    def woven(mine, theirs):
        first = jnp.where(side == 0, mine, theirs).reshape(-1, 1, piece, rows)
        second = jnp.where(side == 0, theirs, mine).reshape(-1, 1, piece, rows)
        return jnp.concatenate([first, second], 1).reshape(2 * cols, rows)

    pair = jnp.concatenate([woven(img_wire, img_other), woven(txt_first, txt_other)], 1)
    whole = lax.all_gather(pair, "z", axis=0, tiled=True)
    whole, feat_there = lax.optimization_barrier((whole, feat_there))
    whole = whole.astype(jnp.float32)

    square = jnp.sum(whole * whole, 0) * (1.0 / WIRE_SCALE**2)
    norm = jnp.sqrt(square + norm_epsilon)
    shrink = 1.0 / (norm * WIRE_SCALE)
    emb = (whole * shrink[None, :]).astype(jnp.bfloat16)
    unit = pair.astype(jnp.float32) * shrink[None, :]
    near = unit.astype(jnp.bfloat16)

    sims = dot(emb[:, :rows], emb[:, rows:], 0, 0)
    place = lax.broadcasted_iota(jnp.int32, (rows, rows), 1)
    positive = (place == partner[:, None]) & (side == 0)
    signs = jnp.where(positive, -1.0, 1.0).astype(jnp.float32)
    coef = (signs * jax.nn.sigmoid(signs * (temper * sims + offset)) * weight).astype(jnp.bfloat16)
    weighted = coef.astype(jnp.float32) * sims
    radial = temper * jnp.concatenate([jnp.sum(weighted, 1), jnp.sum(weighted, 0)])
    def head_side(grad, at, feat):
        part = temper * grad - unit[:, at] * radial[None, at]
        dproj = (part / norm[None, at]).astype(jnp.bfloat16)
        return dot(dproj, feat, 1, 0).astype(jnp.bfloat16)

    img_part = head_side(dot(near[:, rows:], coef, 1, 1), slice(0, rows), img_feat)
    txt_part = head_side(dot(near[:, :rows], coef, 1, 0), slice(rows, None), feat_there)
    part = jnp.concatenate([img_part, txt_part], 0)

    share = lax.all_to_all(part.reshape(count, 2 * piece, -1), near_by, 0, 0, tiled=True)
    share = jnp.sum(share.astype(jnp.float32), 0).astype(jnp.bfloat16).reshape(1, 2, piece, -1)
    share = jnp.broadcast_to(share, (far // 2,) + share.shape[1:]).reshape(far, piece, -1)
    share = lax.all_to_all(share, ("yh", "yl"), 0, 0, tiled=True)
    share = jnp.sum(share.astype(jnp.float32), 0).astype(jnp.bfloat16)
    share = jnp.broadcast_to(share[None], (count,) + share.shape)
    total = lax.all_to_all(share, near_by, 0, 0, tiled=True)
    total = lax.optimization_barrier(total.reshape(2 * cols, -1)).astype(jnp.float32)
    return (total[:cols].T, total[cols:].T)


def solution(mesh):
    lines = Mesh(mesh.devices.reshape(tuple(SIZES.values())), tuple(SIZES))
    return jax.shard_map(
        shards,
        mesh=lines,
        in_specs=(P(DP, None), P(DP, None), P(None, MP), P(None, MP), P(DP), P(), P(), P()),
        out_specs=(P(None, MP), P(None, MP)),
        check_vma=False,
    )
```

```python
import jax
import jax.numpy as jnp
from jax import lax
from jax.sharding import Mesh, PartitionSpec as P

norm_epsilon = 1e-06

DP = ("yh", "x", "core")
MP = ("yl", "z")
SIZES = {"yh": 4, "x": 4, "core": 2, "yl": 2, "z": 12}

WIRE_SCALE = 32.0


def dot(left, right, left_dim, right_dim):
    return lax.dot_general(
        left, right, (((left_dim,), (right_dim,)), ((), ())), preferred_element_type=jnp.float32
    )


def swapped(value, axis):
    return lax.ppermute(value, axis, [(0, 1), (1, 0)])


def from_all(value, axes, routes):
    return lax.ppermute(value, axes, [(b * 2 + s, c * 2 + t) for (b, s), (c, t) in routes])


def shards(img_feat, txt_feat, img_head, txt_head, partner, log_scale, logit_bias, loss_scale):
    rows = img_feat.shape[0]
    cols = img_head.shape[1]
    blocks = lax.axis_size(DP)
    side = lax.axis_index("yl")
    temper = jnp.exp(log_scale[0])
    offset = logit_bias[0]
    weight = loss_scale[0] / (rows * blocks)

    img_wire = (dot(img_head, img_feat, 0, 1) * WIRE_SCALE).astype(jnp.float16)
    txt_wire = (dot(txt_head, txt_feat, 0, 1) * WIRE_SCALE).astype(jnp.float16)

    around = [(b, (b + 1) % blocks) for b in range(blocks)]
    axes = DP + ("yl",)
    txt_other = from_all(
        txt_wire,
        axes,
        [((b, 1), (b, 0)) for b in range(blocks)] + [((b, 0), (c, 1)) for b, c in around],
    )
    txt_before = from_all(txt_wire, axes, [((b, 1), (c, 1)) for b, c in around])
    img_other = swapped(img_wire, "yl")
    txt_first = jnp.where(side == 0, txt_wire, txt_before)

    def in_order(mine, theirs):
        first = jnp.where(side == 0, mine, theirs)
        return jnp.concatenate([first, jnp.where(side == 0, theirs, mine)], 0)

    pair = jnp.concatenate([in_order(img_wire, img_other), in_order(txt_first, txt_other)], 1)
    pair, late_feat = lax.optimization_barrier((pair, txt_feat))
    feat_there = from_all(
        late_feat,
        axes,
        [((b, 0), (b, 0)) for b in range(blocks)] + [((b, 1), (c, 1)) for b, c in around],
    )
    whole = lax.all_gather(pair, "z", axis=0, tiled=True)
    whole, feat_there = lax.optimization_barrier((whole, feat_there))
    whole = whole.astype(jnp.float32)

    square = jnp.sum(whole * whole, 0) * (1.0 / WIRE_SCALE**2)
    norm = jnp.sqrt(square + norm_epsilon)
    shrink = 1.0 / (norm * WIRE_SCALE)
    emb = (whole * shrink[None, :]).astype(jnp.bfloat16)
    unit = pair.astype(jnp.float32) * shrink[None, :]
    near = unit.astype(jnp.bfloat16)

    sims = dot(emb[:, :rows], emb[:, rows:], 0, 0)
    place = lax.broadcasted_iota(jnp.int32, (rows, rows), 1)
    positive = (place == partner[:, None]) & (side == 0)
    signs = jnp.where(positive, -1.0, 1.0).astype(jnp.float32)
    coef = (signs * jax.nn.sigmoid(signs * (temper * sims + offset)) * weight).astype(jnp.bfloat16)
    weighted = coef.astype(jnp.float32) * sims
    radial = temper * jnp.concatenate([jnp.sum(weighted, 1), jnp.sum(weighted, 0)])
    def head_side(grad, at, feat):
        part = temper * grad - unit[:, at] * radial[None, at]
        dproj = (part / norm[None, at]).astype(jnp.bfloat16)
        return dot(dproj, feat, 1, 0).astype(jnp.bfloat16)

    img_part = head_side(dot(near[:, rows:], coef, 1, 1), slice(0, rows), img_feat)
    txt_part = head_side(dot(near[:, :rows], coef, 1, 0), slice(rows, None), feat_there)
    part = jnp.concatenate([img_part[:cols], txt_part[:cols], img_part[cols:], txt_part[cols:]], 0)

    near_by = ("x", "core")
    count, far = lax.axis_size(near_by), lax.axis_size("yh")
    share = part.reshape(2 * count, 2 * cols // count, -1)
    share = lax.all_to_all(share, ("yl",) + near_by, 0, 0, tiled=True)
    share = jnp.sum(share.astype(jnp.float32), 0).astype(jnp.bfloat16)
    share = jnp.broadcast_to(share[None], (far,) + share.shape)
    share = lax.all_to_all(share, "yh", 0, 0, tiled=True)
    share = jnp.sum(share.astype(jnp.float32), 0).astype(jnp.bfloat16)
    share = jnp.broadcast_to(share[None], (count,) + share.shape)
    total = lax.all_to_all(share, near_by, 0, 0, tiled=True)
    total = lax.optimization_barrier(total.reshape(2 * cols, -1)).astype(jnp.float32)
    return (total[:cols].T, total[cols:].T)


def solution(mesh):
    lines = Mesh(mesh.devices.reshape(tuple(SIZES.values())), tuple(SIZES))
    return jax.shard_map(
        shards,
        mesh=lines,
        in_specs=(P(DP, None), P(DP, None), P(None, MP), P(None, MP), P(DP), P(), P(), P()),
        out_specs=(P(None, MP), P(None, MP)),
        check_vma=False,
    )
```

```python
import jax
import jax.numpy as jnp
from jax import lax
from jax.sharding import Mesh, PartitionSpec as P

norm_epsilon = 1e-06

DP = ("yh", "x", "core")
MP = ("yl", "z")
SIZES = {"yh": 4, "x": 4, "core": 2, "yl": 2, "z": 12}

WIRE_SCALE = 32.0


def dot(left, right, left_dim, right_dim):
    return lax.dot_general(
        left, right, (((left_dim,), (right_dim,)), ((), ())), preferred_element_type=jnp.float32
    )


def swapped(value, axis):
    return lax.ppermute(value, axis, [(0, 1), (1, 0)])


def from_all(value, axes, routes):
    return lax.ppermute(value, axes, [(b * 2 + s, c * 2 + t) for (b, s), (c, t) in routes])


def shards(img_feat, txt_feat, img_head, txt_head, partner, log_scale, logit_bias, loss_scale):
    rows = img_feat.shape[0]
    cols = img_head.shape[1]
    blocks = lax.axis_size(DP)
    side = lax.axis_index("yl")
    temper = jnp.exp(log_scale[0])
    offset = logit_bias[0]
    weight = loss_scale[0] / (rows * blocks)

    txt_wire = (dot(txt_head, txt_feat, 0, 1) * WIRE_SCALE).astype(jnp.float16)
    img_wire = (dot(img_head, img_feat, 0, 1) * WIRE_SCALE).astype(jnp.float16)

    around = [(b, (b + 1) % blocks) for b in range(blocks)]
    axes = DP + ("yl",)
    txt_other = from_all(
        txt_wire,
        axes,
        [((b, 1), (b, 0)) for b in range(blocks)] + [((b, 0), (c, 1)) for b, c in around],
    )
    txt_before = from_all(txt_wire, axes, [((b, 1), (c, 1)) for b, c in around])
    img_other = swapped(img_wire, "yl")
    txt_first = jnp.where(side == 0, txt_wire, txt_before)

    pair = jnp.concatenate(
        [
            jnp.concatenate([img_wire, img_other], 0),
            jnp.concatenate([txt_first, txt_other], 0),
        ],
        1,
    )
    whole = lax.all_gather(pair, "z", axis=0, tiled=True)
    whole = whole.astype(jnp.float32)

    square = jnp.sum(whole * whole, 0) * (1.0 / WIRE_SCALE**2)
    norm = jnp.sqrt(square + norm_epsilon)
    shrink = 1.0 / (norm * WIRE_SCALE)
    emb = (whole * shrink[None, :]).astype(jnp.bfloat16)
    unit = pair.astype(jnp.float32) * shrink[None, :]
    near = unit.astype(jnp.bfloat16)

    sims = dot(emb[:, :rows], emb[:, rows:], 0, 0)
    place = lax.broadcasted_iota(jnp.int32, (rows, rows), 1)
    positive = (place == partner[:, None]) & (side == 0)
    signs = jnp.where(positive, -1.0, 1.0).astype(jnp.float32)
    coef = (signs * jax.nn.sigmoid(signs * (temper * sims + offset)) * weight).astype(jnp.bfloat16)
    weighted = coef.astype(jnp.float32) * sims
    radial = temper * jnp.concatenate([jnp.sum(weighted, 1), jnp.sum(weighted, 0)])
    def head_side(grad, at):
        part = temper * grad - unit[:, at] * radial[None, at]
        return (part / norm[None, at]).astype(jnp.bfloat16)

    def by_side(term):
        turned = jnp.concatenate([term[cols:], term[:cols]], 0)
        return jnp.where(side == 0, term, turned)

    txt_term = head_side(dot(near[:, :rows], coef, 1, 0), slice(rows, None))
    txt_after = from_all(txt_term, axes, [((c, 1), (b, 1)) for b, c in around])
    later_coef, txt_term = lax.optimization_barrier((coef, txt_term))
    img_term = head_side(dot(near[:, rows:], later_coef, 1, 1), slice(0, rows))
    img_part = dot(by_side(img_term), img_feat, 1, 0).astype(jnp.bfloat16)
    txt_term = jnp.where(side == 0, txt_term, txt_after)
    txt_part = dot(by_side(txt_term), txt_feat, 1, 0).astype(jnp.bfloat16)
    part = jnp.concatenate([img_part[:cols], txt_part[:cols], img_part[cols:], txt_part[cols:]], 0)

    near_by = ("x", "core")
    count, far = lax.axis_size(near_by), lax.axis_size("yh")
    share = part.reshape(2 * count, 2 * cols // count, -1)
    share = lax.all_to_all(share, ("yl",) + near_by, 0, 0, tiled=True)
    share = jnp.sum(share.astype(jnp.float32), 0).astype(jnp.bfloat16)
    share = jnp.broadcast_to(share[None], (far,) + share.shape)
    share = lax.all_to_all(share, "yh", 0, 0, tiled=True)
    share = jnp.sum(share.astype(jnp.float32), 0).astype(jnp.bfloat16)
    share = jnp.broadcast_to(share[None], (count,) + share.shape)
    total = lax.all_to_all(share, near_by, 0, 0, tiled=True)
    total = lax.optimization_barrier(total.reshape(2 * cols, -1)).astype(jnp.float32)
    return (total[:cols].T, total[cols:].T)


def solution(mesh):
    lines = Mesh(mesh.devices.reshape(tuple(SIZES.values())), tuple(SIZES))
    return jax.shard_map(
        shards,
        mesh=lines,
        in_specs=(P(DP, None), P(DP, None), P(None, MP), P(None, MP), P(DP), P(), P(), P()),
        out_specs=(P(None, MP), P(None, MP)),
        check_vma=False,
    )
```

```python
import jax
import jax.numpy as jnp
from jax import lax
from jax.sharding import Mesh, PartitionSpec as P

norm_epsilon = 1e-06

DP = ("yh", "x", "core")
MP = ("yl", "z")
SIZES = {"yh": 4, "x": 4, "core": 2, "yl": 2, "z": 12}

WIRE_SCALE = 32.0


def dot(left, right, left_dim, right_dim):
    return lax.dot_general(
        left, right, (((left_dim,), (right_dim,)), ((), ())), preferred_element_type=jnp.float32
    )


def swapped(value, axis):
    return lax.ppermute(value, axis, [(0, 1), (1, 0)])


def from_all(value, axes, routes):
    return lax.ppermute(value, axes, [(b * 2 + s, c * 2 + t) for (b, s), (c, t) in routes])


def shards(img_feat, txt_feat, img_head, txt_head, partner, log_scale, logit_bias, loss_scale):
    rows = img_feat.shape[0]
    cols = img_head.shape[1]
    blocks = lax.axis_size(DP)
    side = lax.axis_index("yl")
    temper = jnp.exp(log_scale[0])
    offset = logit_bias[0]
    weight = loss_scale[0] / (rows * blocks)

    txt_wire = (dot(txt_head, txt_feat, 0, 1) * WIRE_SCALE).astype(jnp.float16)
    img_wire = (dot(img_head, img_feat, 0, 1) * WIRE_SCALE).astype(jnp.float16)

    around = [(b, (b + 1) % blocks) for b in range(blocks)]
    axes = DP + ("yl",)
    txt_other = from_all(
        txt_wire,
        axes,
        [((b, 1), (b, 0)) for b in range(blocks)] + [((b, 0), (c, 1)) for b, c in around],
    )
    txt_before = from_all(txt_wire, axes, [((b, 1), (c, 1)) for b, c in around])
    img_other = swapped(img_wire, "yl")
    txt_first = jnp.where(side == 0, txt_wire, txt_before)
    txt_other, img_other = lax.optimization_barrier((txt_other, img_other))

    pair = jnp.concatenate(
        [
            jnp.concatenate([img_wire, img_other], 0),
            jnp.concatenate([txt_first, txt_other], 0),
        ],
        1,
    )
    whole = lax.all_gather(pair, "z", axis=0, tiled=True)
    whole = whole.astype(jnp.float32)

    square = jnp.sum(whole * whole, 0) * (1.0 / WIRE_SCALE**2)
    norm = jnp.sqrt(square + norm_epsilon)
    shrink = 1.0 / (norm * WIRE_SCALE)
    emb = (whole * shrink[None, :]).astype(jnp.bfloat16)
    unit = pair.astype(jnp.float32) * shrink[None, :]
    near = unit.astype(jnp.bfloat16)

    sims = dot(emb[:, :rows], emb[:, rows:], 0, 0)
    place = lax.broadcasted_iota(jnp.int32, (rows, rows), 1)
    positive = (place == partner[:, None]) & (side == 0)
    signs = jnp.where(positive, -1.0, 1.0).astype(jnp.float32)
    coef = (signs * jax.nn.sigmoid(signs * (temper * sims + offset)) * weight).astype(jnp.bfloat16)
    weighted = coef.astype(jnp.float32) * sims
    radial = temper * jnp.concatenate([jnp.sum(weighted, 1), jnp.sum(weighted, 0)])
    def head_side(grad, at):
        part = temper * grad - unit[:, at] * radial[None, at]
        return (part / norm[None, at]).astype(jnp.bfloat16)

    def by_side(term):
        turned = jnp.concatenate([term[cols:], term[:cols]], 0)
        return jnp.where(side == 0, term, turned)

    txt_term = head_side(dot(near[:, :rows], coef, 1, 0), slice(rows, None))
    txt_after = from_all(txt_term, axes, [((c, 1), (b, 1)) for b, c in around])
    later_coef, txt_term = lax.optimization_barrier((coef, txt_term))
    img_term = head_side(dot(near[:, rows:], later_coef, 1, 1), slice(0, rows))
    img_part = dot(by_side(img_term), img_feat, 1, 0).astype(jnp.bfloat16)
    txt_term = jnp.where(side == 0, txt_term, txt_after)
    txt_part = dot(by_side(txt_term), txt_feat, 1, 0).astype(jnp.bfloat16)
    part = jnp.concatenate([img_part[:cols], txt_part[:cols], img_part[cols:], txt_part[cols:]], 0)

    near_by = ("x", "core")
    count, far = lax.axis_size(near_by), lax.axis_size("yh")
    share = part.reshape(2 * count, 2 * cols // count, -1)
    share = lax.all_to_all(share, ("yl",) + near_by, 0, 0, tiled=True)
    share = jnp.sum(share.astype(jnp.float32), 0).astype(jnp.bfloat16)
    share = jnp.broadcast_to(share[None], (far,) + share.shape)
    share = lax.all_to_all(share, "yh", 0, 0, tiled=True)
    share = jnp.sum(share.astype(jnp.float32), 0).astype(jnp.bfloat16)
    share = jnp.broadcast_to(share[None], (count,) + share.shape)
    total = lax.all_to_all(share, near_by, 0, 0, tiled=True)
    total = lax.optimization_barrier(total.reshape(2 * cols, -1)).astype(jnp.float32)
    return (total[:cols].T, total[cols:].T)


def solution(mesh):
    lines = Mesh(mesh.devices.reshape(tuple(SIZES.values())), tuple(SIZES))
    return jax.shard_map(
        shards,
        mesh=lines,
        in_specs=(P(DP, None), P(DP, None), P(None, MP), P(None, MP), P(DP), P(), P(), P()),
        out_specs=(P(None, MP), P(None, MP)),
        check_vma=False,
    )
```

```python
import jax
import jax.numpy as jnp
from jax import lax
from jax.sharding import Mesh, PartitionSpec as P

norm_epsilon = 1e-06

DP = ("yh", "x", "core")
MP = ("yl", "z")
SIZES = {"yh": 4, "x": 4, "core": 2, "yl": 2, "z": 12}

WIRE_SCALE = 32.0


def dot(left, right, left_dim, right_dim):
    return lax.dot_general(
        left, right, (((left_dim,), (right_dim,)), ((), ())), preferred_element_type=jnp.float32
    )


def swapped(value, axis):
    return lax.ppermute(value, axis, [(0, 1), (1, 0)])


def from_all(value, axes, routes):
    return lax.ppermute(value, axes, [(b * 2 + s, c * 2 + t) for (b, s), (c, t) in routes])


def shards(img_feat, txt_feat, img_head, txt_head, partner, log_scale, logit_bias, loss_scale):
    rows = img_feat.shape[0]
    cols = img_head.shape[1]
    blocks = lax.axis_size(DP)
    side = lax.axis_index("yl")
    temper = jnp.exp(log_scale[0])
    offset = logit_bias[0]
    weight = loss_scale[0] / (rows * blocks)

    txt_wire = (dot(txt_head, txt_feat, 0, 1) * WIRE_SCALE).astype(jnp.float16)
    img_wire = (dot(img_head, img_feat, 0, 1) * WIRE_SCALE).astype(jnp.float16)

    around = [(b, (b + 1) % blocks) for b in range(blocks)]
    axes = DP + ("yl",)
    txt_other = from_all(
        txt_wire,
        axes,
        [((b, 1), (b, 0)) for b in range(blocks)] + [((b, 0), (c, 1)) for b, c in around],
    )
    txt_before = from_all(txt_wire, axes, [((b, 1), (c, 1)) for b, c in around])
    img_other = swapped(img_wire, "yl")
    txt_other, txt_before = lax.optimization_barrier((txt_other, txt_before))
    txt_first = jnp.where(side == 0, txt_wire, txt_before)

    pair = jnp.concatenate(
        [
            jnp.concatenate([img_wire, img_other], 0),
            jnp.concatenate([txt_first, txt_other], 0),
        ],
        1,
    )
    whole = lax.all_gather(pair, "z", axis=0, tiled=True)
    whole = whole.astype(jnp.float32)

    square = jnp.sum(whole * whole, 0) * (1.0 / WIRE_SCALE**2)
    norm = jnp.sqrt(square + norm_epsilon)
    shrink = 1.0 / (norm * WIRE_SCALE)
    emb = (whole * shrink[None, :]).astype(jnp.bfloat16)
    unit = pair.astype(jnp.float32) * shrink[None, :]
    near = unit.astype(jnp.bfloat16)

    sims = dot(emb[:, :rows], emb[:, rows:], 0, 0)
    place = lax.broadcasted_iota(jnp.int32, (rows, rows), 1)
    positive = (place == partner[:, None]) & (side == 0)
    signs = jnp.where(positive, -1.0, 1.0).astype(jnp.float32)
    coef = (signs * jax.nn.sigmoid(signs * (temper * sims + offset)) * weight).astype(jnp.bfloat16)
    weighted = coef.astype(jnp.float32) * sims
    radial = temper * jnp.concatenate([jnp.sum(weighted, 1), jnp.sum(weighted, 0)])
    def head_side(grad, at):
        part = temper * grad - unit[:, at] * radial[None, at]
        return (part / norm[None, at]).astype(jnp.bfloat16)

    def by_side(term):
        turned = jnp.concatenate([term[cols:], term[:cols]], 0)
        return jnp.where(side == 0, term, turned)

    txt_term = head_side(dot(near[:, :rows], coef, 1, 0), slice(rows, None))
    txt_after = from_all(txt_term, axes, [((c, 1), (b, 1)) for b, c in around])
    later_coef, txt_term = lax.optimization_barrier((coef, txt_term))
    img_term = head_side(dot(near[:, rows:], later_coef, 1, 1), slice(0, rows))
    img_part = dot(by_side(img_term), img_feat, 1, 0).astype(jnp.bfloat16)
    txt_term = jnp.where(side == 0, txt_term, txt_after)
    txt_part = dot(by_side(txt_term), txt_feat, 1, 0).astype(jnp.bfloat16)
    part = jnp.concatenate([img_part[:cols], txt_part[:cols], img_part[cols:], txt_part[cols:]], 0)

    near_by = ("x", "core")
    count, far = lax.axis_size(near_by), lax.axis_size("yh")
    share = part.reshape(2 * count, 2 * cols // count, -1)
    share = lax.all_to_all(share, ("yl",) + near_by, 0, 0, tiled=True)
    share = jnp.sum(share.astype(jnp.float32), 0).astype(jnp.bfloat16)
    share = jnp.broadcast_to(share[None], (far,) + share.shape)
    share = lax.all_to_all(share, "yh", 0, 0, tiled=True)
    share = jnp.sum(share.astype(jnp.float32), 0).astype(jnp.bfloat16)
    share = jnp.broadcast_to(share[None], (count,) + share.shape)
    total = lax.all_to_all(share, near_by, 0, 0, tiled=True)
    total = lax.optimization_barrier(total.reshape(2 * cols, -1)).astype(jnp.float32)
    return (total[:cols].T, total[cols:].T)


def solution(mesh):
    lines = Mesh(mesh.devices.reshape(tuple(SIZES.values())), tuple(SIZES))
    return jax.shard_map(
        shards,
        mesh=lines,
        in_specs=(P(DP, None), P(DP, None), P(None, MP), P(None, MP), P(DP), P(), P(), P()),
        out_specs=(P(None, MP), P(None, MP)),
        check_vma=False,
    )
```

```python
import jax
import jax.numpy as jnp
from jax import lax
from jax.sharding import Mesh, PartitionSpec as P

norm_epsilon = 1e-06

DP = ("yh", "x", "core")
MP = ("yl", "z")
SIZES = {"yh": 4, "x": 4, "core": 2, "yl": 2, "z": 12}

WIRE_SCALE = 32.0


def dot(left, right, left_dim, right_dim):
    return lax.dot_general(
        left, right, (((left_dim,), (right_dim,)), ((), ())), preferred_element_type=jnp.float32
    )


def swapped(value, axis):
    return lax.ppermute(value, axis, [(0, 1), (1, 0)])


def from_all(value, axes, routes):
    return lax.ppermute(value, axes, [(b * 2 + s, c * 2 + t) for (b, s), (c, t) in routes])


def shards(img_feat, txt_feat, img_head, txt_head, partner, log_scale, logit_bias, loss_scale):
    rows = img_feat.shape[0]
    cols = img_head.shape[1]
    blocks = lax.axis_size(DP)
    side = lax.axis_index("yl")
    temper = jnp.exp(log_scale[0])
    offset = logit_bias[0]
    weight = loss_scale[0] / (rows * blocks)

    txt_wire = (dot(txt_head, txt_feat, 0, 1) * WIRE_SCALE).astype(jnp.float16)
    img_wire = (dot(img_head, img_feat, 0, 1) * WIRE_SCALE).astype(jnp.float16)

    around = [(b, (b + 1) % blocks) for b in range(blocks)]
    axes = DP + ("yl",)
    txt_other = from_all(
        txt_wire,
        axes,
        [((b, 1), (b, 0)) for b in range(blocks)] + [((b, 0), (c, 1)) for b, c in around],
    )
    txt_before = from_all(txt_wire, axes, [((b, 1), (c, 1)) for b, c in around])
    img_other = swapped(img_wire, "yl")
    txt_other, txt_before = lax.optimization_barrier((txt_other, txt_before))
    txt_first = jnp.where(side == 0, txt_wire, txt_before)

    pair = jnp.concatenate(
        [
            jnp.concatenate([img_wire, img_other], 0),
            jnp.concatenate([txt_first, txt_other], 0),
        ],
        1,
    )
    whole = lax.all_gather(pair, "z", axis=0, tiled=True)
    whole = whole.astype(jnp.float32)

    square = jnp.sum(whole * whole, 0) * (1.0 / WIRE_SCALE**2)
    norm = jnp.sqrt(square + norm_epsilon)
    shrink = 1.0 / (norm * WIRE_SCALE)
    emb = (whole * shrink[None, :]).astype(jnp.bfloat16)
    unit = pair.astype(jnp.float32) * shrink[None, :]
    near = unit.astype(jnp.bfloat16)

    sims = dot(emb[:, :rows], emb[:, rows:], 0, 0)
    place = lax.broadcasted_iota(jnp.int32, (rows, rows), 1)
    positive = (place == partner[:, None]) & (side == 0)
    signs = jnp.where(positive, -1.0, 1.0).astype(jnp.float32)
    coef = (signs * jax.nn.sigmoid(signs * (temper * sims + offset)) * weight).astype(jnp.bfloat16)
    weighted = coef.astype(jnp.float32) * sims
    radial = temper * jnp.concatenate([jnp.sum(weighted, 1), jnp.sum(weighted, 0)])
    def head_side(grad, at):
        part = temper * grad - unit[:, at] * radial[None, at]
        return (part / norm[None, at]).astype(jnp.bfloat16)

    def by_side(term):
        turned = jnp.concatenate([term[cols:], term[:cols]], 0)
        return jnp.where(side == 0, term, turned)

    txt_term = head_side(dot(near[:, :rows], coef, 1, 0), slice(rows, None))
    txt_after = from_all(txt_term, axes, [((c, 1), (b, 1)) for b, c in around])
    later_coef, txt_term = lax.optimization_barrier((coef, txt_term))
    img_term = head_side(dot(near[:, rows:], later_coef, 1, 1), slice(0, rows))
    img_part = dot(by_side(img_term), img_feat, 1, 0).astype(jnp.bfloat16)
    txt_term = jnp.where(side == 0, txt_term, txt_after)
    txt_part = dot(by_side(txt_term), txt_feat, 1, 0).astype(jnp.bfloat16)
    part = jnp.concatenate([img_part[:cols], txt_part[:cols], img_part[cols:], txt_part[cols:]], 0)

    near_by = ("x", "core")
    count, far = lax.axis_size(near_by), lax.axis_size("yh")
    share = part.reshape(2 * count, 2 * cols // count, -1)
    share = lax.all_to_all(share, ("yl",) + near_by, 0, 0, tiled=True)
    share = jnp.sum(share.astype(jnp.float32), 0).astype(jnp.bfloat16)
    first, second, third, fourth = [share.astype(jnp.float32)] + [
        lax.ppermute(share, "yh", [(i, (i + step) % far) for i in range(far)]).astype(jnp.float32)
        for step in (2, 1, 3)
    ]
    share = ((first + second) + (third + fourth)).astype(jnp.bfloat16)
    share = jnp.broadcast_to(share[None], (count,) + share.shape)
    total = lax.all_to_all(share, near_by, 0, 0, tiled=True)
    total = lax.optimization_barrier(total.reshape(2 * cols, -1)).astype(jnp.float32)
    return (total[:cols].T, total[cols:].T)


def solution(mesh):
    lines = Mesh(mesh.devices.reshape(tuple(SIZES.values())), tuple(SIZES))
    return jax.shard_map(
        shards,
        mesh=lines,
        in_specs=(P(DP, None), P(DP, None), P(None, MP), P(None, MP), P(DP), P(), P(), P()),
        out_specs=(P(None, MP), P(None, MP)),
        check_vma=False,
    )
```

```python
import jax
import jax.numpy as jnp
from jax import lax
from jax.sharding import Mesh, PartitionSpec as P

norm_epsilon = 1e-06

DP = ("yh", "x", "core")
MP = ("yl", "z")
SIZES = {"yh": 4, "x": 4, "core": 2, "yl": 2, "z": 12}

WIRE_SCALE = 32.0


def dot(left, right, left_dim, right_dim):
    return lax.dot_general(
        left, right, (((left_dim,), (right_dim,)), ((), ())), preferred_element_type=jnp.float32
    )


def swapped(value, axis):
    return lax.ppermute(value, axis, [(0, 1), (1, 0)])


def from_all(value, axes, routes):
    return lax.ppermute(value, axes, [(b * 2 + s, c * 2 + t) for (b, s), (c, t) in routes])


def shards(img_feat, txt_feat, img_head, txt_head, partner, log_scale, logit_bias, loss_scale):
    rows = img_feat.shape[0]
    cols = img_head.shape[1]
    blocks = lax.axis_size(DP)
    side = lax.axis_index("yl")
    temper = jnp.exp(log_scale[0])
    offset = logit_bias[0]
    weight = loss_scale[0] / (rows * blocks)

    txt_wire = (dot(txt_head, txt_feat, 0, 1) * WIRE_SCALE).astype(jnp.float16)
    img_wire = (dot(img_head, img_feat, 0, 1) * WIRE_SCALE).astype(jnp.float16)

    around = [(b, (b + 1) % blocks) for b in range(blocks)]
    axes = DP + ("yl",)
    txt_other = from_all(
        txt_wire,
        axes,
        [((b, 1), (b, 0)) for b in range(blocks)] + [((b, 0), (c, 1)) for b, c in around],
    )
    txt_before = from_all(txt_wire, axes, [((b, 1), (c, 1)) for b, c in around])
    img_other = swapped(img_wire, "yl")
    txt_first = jnp.where(side == 0, txt_wire, txt_before)
    txt_other, img_other = lax.optimization_barrier((txt_other, img_other))

    pair = jnp.concatenate(
        [
            jnp.concatenate([img_wire, img_other], 0),
            jnp.concatenate([txt_first, txt_other], 0),
        ],
        1,
    )
    whole = lax.all_gather(pair, "z", axis=0, tiled=True)
    whole = whole.astype(jnp.float32)

    square = jnp.sum(whole * whole, 0) * (1.0 / WIRE_SCALE**2)
    norm = jnp.sqrt(square + norm_epsilon)
    shrink = 1.0 / (norm * WIRE_SCALE)
    emb = (whole * shrink[None, :]).astype(jnp.bfloat16)
    unit = pair.astype(jnp.float32) * shrink[None, :]
    near = unit.astype(jnp.bfloat16)

    sims = dot(emb[:, :rows], emb[:, rows:], 0, 0)
    place = lax.broadcasted_iota(jnp.int32, (rows, rows), 1)
    positive = (place == partner[:, None]) & (side == 0)
    signs = jnp.where(positive, -1.0, 1.0).astype(jnp.float32)
    coef = (signs * jax.nn.sigmoid(signs * (temper * sims + offset)) * weight).astype(jnp.bfloat16)
    weighted = coef.astype(jnp.float32) * sims
    radial = temper * jnp.concatenate([jnp.sum(weighted, 1), jnp.sum(weighted, 0)])
    def head_side(grad, at):
        part = temper * grad - unit[:, at] * radial[None, at]
        return (part / norm[None, at]).astype(jnp.bfloat16)

    def by_side(term):
        turned = jnp.concatenate([term[cols:], term[:cols]], 0)
        return jnp.where(side == 0, term, turned)

    txt_term = head_side(dot(near[:, :rows], coef, 1, 0), slice(rows, None))
    txt_after = from_all(txt_term, axes, [((c, 1), (b, 1)) for b, c in around])
    later_coef, txt_term = lax.optimization_barrier((coef, txt_term))
    img_term = head_side(dot(near[:, rows:], later_coef, 1, 1), slice(0, rows))
    img_part = dot(by_side(img_term), img_feat, 1, 0).astype(jnp.bfloat16)
    txt_term = jnp.where(side == 0, txt_term, txt_after)
    txt_part = dot(by_side(txt_term), txt_feat, 1, 0).astype(jnp.bfloat16)
    near_by = ("x", "core")
    count, far = lax.axis_size(near_by), lax.axis_size("yh")
    down, along = 2 * cols // 8, img_part.shape[1] // 128
    each = -(-down * along // count) * 8
    spare = ((0, count * each - down * along * 8), (0, 0))

    def tiled(at):
        rows_of = jnp.concatenate([img_part[at], txt_part[at]], 0)
        rows_of = rows_of.reshape(down, 8, along, 128).transpose(0, 2, 1, 3)
        return jnp.pad(rows_of.reshape(-1, 128), spare)

    share = jnp.concatenate([tiled(slice(0, cols)), tiled(slice(cols, None))], 0)
    share = share.reshape(2 * count, each, 128)
    share = lax.all_to_all(share, ("yl",) + near_by, 0, 0, tiled=True)
    share = jnp.sum(share.astype(jnp.float32), 0).astype(jnp.bfloat16)
    share = jnp.broadcast_to(share[None], (far,) + share.shape)
    share = lax.all_to_all(share, "yh", 0, 0, tiled=True)
    share = jnp.sum(share.astype(jnp.float32), 0).astype(jnp.bfloat16)
    share = jnp.broadcast_to(share[None], (count,) + share.shape)
    total = lax.all_to_all(share, near_by, 0, 0, tiled=True).reshape(-1, 128)
    total = total[: down * along * 8].astype(jnp.float32)
    total = total.reshape(down, along, 8, 128).transpose(0, 2, 1, 3).reshape(2 * cols, -1)
    return (total[:cols].T, total[cols:].T)


def solution(mesh):
    lines = Mesh(mesh.devices.reshape(tuple(SIZES.values())), tuple(SIZES))
    return jax.shard_map(
        shards,
        mesh=lines,
        in_specs=(P(DP, None), P(DP, None), P(None, MP), P(None, MP), P(DP), P(), P(), P()),
        out_specs=(P(None, MP), P(None, MP)),
        check_vma=False,
    )
```

```python
import jax
import jax.numpy as jnp
from jax import lax
from jax.sharding import Mesh, PartitionSpec as P

norm_epsilon = 1e-06

DP = ("yh", "x", "core")
MP = ("yl", "z")
SIZES = {"yh": 4, "x": 4, "core": 2, "yl": 2, "z": 12}

WIRE_SCALE = 32.0


def dot(left, right, left_dim, right_dim):
    return lax.dot_general(
        left, right, (((left_dim,), (right_dim,)), ((), ())), preferred_element_type=jnp.float32
    )


def swapped(value, axis):
    return lax.ppermute(value, axis, [(0, 1), (1, 0)])


def from_all(value, axes, routes):
    return lax.ppermute(value, axes, [(b * 2 + s, c * 2 + t) for (b, s), (c, t) in routes])


def shards(img_feat, txt_feat, img_head, txt_head, partner, log_scale, logit_bias, loss_scale):
    rows = img_feat.shape[0]
    cols = img_head.shape[1]
    blocks = lax.axis_size(DP)
    side = lax.axis_index("yl")
    temper = jnp.exp(log_scale[0])
    offset = logit_bias[0]
    weight = loss_scale[0] / (rows * blocks)

    txt_wire = (dot(txt_head, txt_feat, 0, 1) * WIRE_SCALE).astype(jnp.float16)
    img_wire = (dot(img_head, img_feat, 0, 1) * WIRE_SCALE).astype(jnp.float16)

    around = [(b, (b + 1) % blocks) for b in range(blocks)]
    axes = DP + ("yl",)
    txt_other = from_all(
        txt_wire,
        axes,
        [((b, 1), (b, 0)) for b in range(blocks)] + [((b, 0), (c, 1)) for b, c in around],
    )
    txt_before = from_all(txt_wire, axes, [((b, 1), (c, 1)) for b, c in around])
    img_other = swapped(img_wire, "yl")
    txt_other, txt_before = lax.optimization_barrier((txt_other, txt_before))
    txt_first = jnp.where(side == 0, txt_wire, txt_before)

    pair = jnp.concatenate(
        [
            jnp.concatenate([img_wire, img_other], 0),
            jnp.concatenate([txt_first, txt_other], 0),
        ],
        1,
    )
    whole = lax.all_gather(pair, "z", axis=0, tiled=True)
    whole = whole.astype(jnp.float32)

    square = jnp.sum(whole * whole, 0) * (1.0 / WIRE_SCALE**2)
    norm = jnp.sqrt(square + norm_epsilon)
    shrink = 1.0 / (norm * WIRE_SCALE)
    emb = (whole * shrink[None, :]).astype(jnp.bfloat16)
    unit = pair.astype(jnp.float32) * shrink[None, :]
    near = unit.astype(jnp.bfloat16)

    sims = dot(emb[:, :rows], emb[:, rows:], 0, 0)
    place = lax.broadcasted_iota(jnp.int32, (rows, rows), 1)
    positive = (place == partner[:, None]) & (side == 0)
    signs = jnp.where(positive, -1.0, 1.0).astype(jnp.float32)
    coef = (signs * jax.nn.sigmoid(signs * (temper * sims + offset)) * weight).astype(jnp.bfloat16)
    weighted = coef.astype(jnp.float32) * sims
    radial = temper * jnp.concatenate([jnp.sum(weighted, 1), jnp.sum(weighted, 0)])
    def head_side(grad, at):
        part = temper * grad - unit[:, at] * radial[None, at]
        return (part / norm[None, at]).astype(jnp.bfloat16)

    def by_side(term):
        turned = jnp.concatenate([term[cols:], term[:cols]], 0)
        return jnp.where(side == 0, term, turned)

    txt_term = head_side(dot(near[:, :rows], coef, 1, 0), slice(rows, None))
    txt_after = from_all(txt_term, axes, [((c, 1), (b, 1)) for b, c in around])
    later_coef, txt_term = lax.optimization_barrier((coef, txt_term))
    img_term = head_side(dot(near[:, rows:], later_coef, 1, 1), slice(0, rows))
    img_part = dot(by_side(img_term), img_feat, 1, 0).astype(jnp.bfloat16)
    txt_term = jnp.where(side == 0, txt_term, txt_after)
    txt_part = dot(by_side(txt_term), txt_feat, 1, 0).astype(jnp.bfloat16)
    near_by = ("x", "core")
    count, far = lax.axis_size(near_by), lax.axis_size("yh")
    down, along = 2 * cols // 8, img_part.shape[1] // 128
    each = -(-down * along // count) * 8
    spare = ((0, count * each - down * along * 8), (0, 0))

    def tiled(at):
        rows_of = jnp.concatenate([img_part[at], txt_part[at]], 0)
        rows_of = rows_of.reshape(down, 8, along, 128).transpose(0, 2, 1, 3)
        return jnp.pad(rows_of.reshape(-1, 128), spare)

    share = jnp.concatenate([tiled(slice(0, cols)), tiled(slice(cols, None))], 0)
    share = share.reshape(2 * count, each, 128)
    share = lax.all_to_all(share, ("yl",) + near_by, 0, 0, tiled=True)
    share = jnp.sum(share.astype(jnp.float32), 0).astype(jnp.bfloat16)
    share = jnp.broadcast_to(share[None], (far,) + share.shape)
    share = lax.all_to_all(share, "yh", 0, 0, tiled=True)
    share = jnp.sum(share.astype(jnp.float32), 0).astype(jnp.bfloat16)
    share = jnp.broadcast_to(share[None], (count,) + share.shape)
    total = lax.all_to_all(share, near_by, 0, 0, tiled=True).reshape(-1, 128)
    total = total[: down * along * 8].astype(jnp.float32)
    total = total.reshape(down, along, 8, 128).transpose(0, 2, 1, 3).reshape(2 * cols, -1)
    return (total[:cols].T, total[cols:].T)


def solution(mesh):
    lines = Mesh(mesh.devices.reshape(tuple(SIZES.values())), tuple(SIZES))
    return jax.shard_map(
        shards,
        mesh=lines,
        in_specs=(P(DP, None), P(DP, None), P(None, MP), P(None, MP), P(DP), P(), P(), P()),
        out_specs=(P(None, MP), P(None, MP)),
        check_vma=False,
    )
```

```python
import jax
import jax.numpy as jnp
from jax import lax
from jax.sharding import Mesh, PartitionSpec as P

norm_epsilon = 1e-06

DP = ("yh", "x", "core")
MP = ("yl", "z")
SIZES = {"yh": 4, "x": 4, "core": 2, "yl": 2, "z": 12}

WIRE_SCALE = 32.0


def dot(left, right, left_dim, right_dim):
    return lax.dot_general(
        left, right, (((left_dim,), (right_dim,)), ((), ())), preferred_element_type=jnp.float32
    )


def swapped(value, axis):
    return lax.ppermute(value, axis, [(0, 1), (1, 0)])


def from_all(value, axes, routes):
    return lax.ppermute(value, axes, [(b * 2 + s, c * 2 + t) for (b, s), (c, t) in routes])


def shards(img_feat, txt_feat, img_head, txt_head, partner, log_scale, logit_bias, loss_scale):
    rows = img_feat.shape[0]
    cols = img_head.shape[1]
    blocks = lax.axis_size(DP)
    side = lax.axis_index("yl")
    temper = jnp.exp(log_scale[0])
    offset = logit_bias[0]
    weight = loss_scale[0] / (rows * blocks)

    txt_wire = (dot(txt_head, txt_feat, 0, 1) * WIRE_SCALE).astype(jnp.float16)
    img_wire = (dot(img_head, img_feat, 0, 1) * WIRE_SCALE).astype(jnp.float16)

    around = [(b, (b + 1) % blocks) for b in range(blocks)]
    axes = DP + ("yl",)
    txt_other = from_all(
        txt_wire,
        axes,
        [((b, 1), (b, 0)) for b in range(blocks)] + [((b, 0), (c, 1)) for b, c in around],
    )
    txt_before = from_all(txt_wire, axes, [((b, 1), (c, 1)) for b, c in around])
    img_other = swapped(img_wire, "yl")
    txt_first = jnp.where(side == 0, txt_wire, txt_before)
    txt_other, img_other = lax.optimization_barrier((txt_other, img_other))

    pair = jnp.concatenate(
        [
            jnp.concatenate([img_wire, img_other], 0),
            jnp.concatenate([txt_first, txt_other], 0),
        ],
        1,
    )
    whole = lax.all_gather(pair, "z", axis=0, tiled=True)
    whole = whole.astype(jnp.float32)

    square = jnp.sum(whole * whole, 0) * (1.0 / WIRE_SCALE**2)
    norm = jnp.sqrt(square + norm_epsilon)
    shrink = 1.0 / (norm * WIRE_SCALE)
    emb = (whole * shrink[None, :]).astype(jnp.bfloat16)
    unit = pair.astype(jnp.float32) * shrink[None, :]
    near = unit.astype(jnp.bfloat16)

    sims = dot(emb[:, :rows], emb[:, rows:], 0, 0)
    place = lax.broadcasted_iota(jnp.int32, (rows, rows), 1)
    positive = (place == partner[:, None]) & (side == 0)
    signs = jnp.where(positive, -1.0, 1.0).astype(jnp.float32)
    coef = (signs * jax.nn.sigmoid(signs * (temper * sims + offset)) * weight).astype(jnp.bfloat16)
    weighted = coef.astype(jnp.float32) * sims
    radial = temper * jnp.concatenate([jnp.sum(weighted, 1), jnp.sum(weighted, 0)])
    def head_side(grad, at):
        part = temper * grad - unit[:, at] * radial[None, at]
        return (part / norm[None, at]).astype(jnp.bfloat16)

    def by_side(term):
        turned = jnp.concatenate([term[cols:], term[:cols]], 0)
        return jnp.where(side == 0, term, turned)

    txt_term = head_side(dot(near[:, :rows], coef, 1, 0), slice(rows, None))
    txt_after = from_all(txt_term, axes, [((c, 1), (b, 1)) for b, c in around])
    later_coef, txt_term = lax.optimization_barrier((coef, txt_term))
    img_term = head_side(dot(near[:, rows:], later_coef, 1, 1), slice(0, rows))
    img_part = dot(by_side(img_term), img_feat, 1, 0).astype(jnp.bfloat16)
    txt_term = jnp.where(side == 0, txt_term, txt_after)
    txt_part = dot(by_side(txt_term), txt_feat, 1, 0).astype(jnp.bfloat16)
    near_by = ("x", "core")
    count, far = lax.axis_size(near_by), lax.axis_size("yh")
    down, along = 2 * cols // 8, img_part.shape[1] // 128
    each = -(-down * along // count) * 8
    spare = ((0, count * each - down * along * 8), (0, 0))

    def tiled(at):
        rows_of = jnp.concatenate([img_part[at], txt_part[at]], 0)
        rows_of = rows_of.reshape(down, 8, along, 128).transpose(0, 2, 1, 3)
        return jnp.pad(rows_of.reshape(-1, 128), spare)

    share = jnp.concatenate([tiled(slice(0, cols)), tiled(slice(cols, None))], 0)
    share = share.reshape(2 * count, each, 128)
    share = lax.all_to_all(share, ("yl",) + near_by, 0, 0, tiled=True)
    share = jnp.sum(share.astype(jnp.float32), 0).astype(jnp.bfloat16)
    share = jnp.broadcast_to(share[None], (far,) + share.shape)
    share = lax.all_to_all(share, "yh", 0, 0, tiled=True)
    share = jnp.sum(share.astype(jnp.float32), 0).astype(jnp.bfloat16)
    share = jnp.broadcast_to(share[None], (count,) + share.shape)
    total = lax.all_to_all(share, near_by, 0, 0, tiled=True).reshape(-1, 128)
    size = down * along * 4

    def head(tiles):
        tiles = tiles.reshape(down // 2, along, 8, 128).transpose(0, 2, 1, 3)
        return tiles.reshape(cols, -1).astype(jnp.float32).T

    return (head(total[:size]), head(total[size : 2 * size]))


def solution(mesh):
    lines = Mesh(mesh.devices.reshape(tuple(SIZES.values())), tuple(SIZES))
    return jax.shard_map(
        shards,
        mesh=lines,
        in_specs=(P(DP, None), P(DP, None), P(None, MP), P(None, MP), P(DP), P(), P(), P()),
        out_specs=(P(None, MP), P(None, MP)),
        check_vma=False,
    )
```
